512 devices in a mesh: pipe: 64 (over z, y_hi, core), tensor: 8 (over y_lo, x).
Axes of the slice: x: 4, y: 8 (y_hi: 4, y_lo: 2; y = y_hi * 2 + y_lo), z: 8, core: 2. Of those that a mesh axis runs over, the one named last changes fastest.
Arguments:
- fwd_queries: bfloat16 [64, 352, 8192], P('pipe', None, 'tensor'), may hold values from -100 to 100, as said below
- fwd_kv: bfloat16 [64, 2, 352, 1024], P('pipe', None, None, 'tensor'), may hold values from -6 to 6
- fwd_resid: bfloat16 [64, 352, 8192], P('pipe', None, 'tensor'), may hold values from -6 to 6
- fwd_bounds: int32 [64], P('pipe'), may hold values from 1 to 351
- gain: bfloat16 [8192], P('tensor'), may hold values from 0.099609375 to 1.8984375
- stash_queries: bfloat16 [64, 352, 8192], P('pipe', None, 'tensor'), may hold values from -100 to 100, as said below
- stash_kv: bfloat16 [64, 2, 352, 1024], P('pipe', None, None, 'tensor'), may hold values from -6 to 6
- stash_bounds: int32 [64], P('pipe'), may hold values from 1 to 351
- grad_out: bfloat16 [64, 352, 8192], P('pipe', None, 'tensor'), may hold values from -6 to 6
Outputs:
- normed: bfloat16 [64, 352, 8192], P('pipe', None, 'tensor')
- grad_queries: bfloat16 [64, 352, 8192], P('pipe', None, 'tensor')
- grad_kv: bfloat16 [64, 2, 352, 1024], P('pipe', None, None, 'tensor')
The draws below stay inside these ranges and needn't reach their ends.
Inputs may be any that keep to these rules, and one draw needn't show every extreme that they name: `fwd_queries`: queries reach at most 100 in magnitude. `stash_queries`: queries reach at most 100 in magnitude.
All inputs are finite; a program needn't handle non-finite values.
Results may differ from the reference program's by a relative error of at most 0.005.
Values may be sent and summed in bfloat16 or wider, within the bound.
No kernel may reach another device: no remote copies, remote signals or barrier semaphores. Data moves between devices by JAX's collectives and lax.ppermute only.
A program may use at most 64 MiB of HBM per device.

```python
import jax
import jax.numpy as jnp
from jax import lax

HEADS = 64
KVH = 8
HD = 128
TOK = 352
D = 8192
SECTIONS = 64


def shared_keys(key, salt):
    return jax.random.normal(jax.random.fold_in(key, salt), (SECTIONS, TOK, KVH * HD), jnp.float32)


def query_draw(key, own):
    inner = jax.random.fold_in(key, own)
    base = jax.random.normal(inner, (SECTIONS, TOK, HEADS, HD), jnp.float32)
    base = jnp.clip(base, -6.0, 6.0)
    return base.reshape(SECTIONS, TOK, HEADS * HD).astype(jnp.bfloat16)


def pair_draw(key, salt, own):
    keys = jnp.clip(shared_keys(key, salt), -6.0, 6.0)
    inner = jax.random.fold_in(key, own)
    values = jnp.clip(jax.random.normal(inner, (SECTIONS, TOK, KVH * HD), jnp.float32), -6.0, 6.0)
    return jnp.stack([keys, values], axis=1).astype(jnp.bfloat16)


def draw_fwd_queries(key, part):
    return query_draw(key, 11)


def draw_fwd_kv(key, part):
    return pair_draw(key, 101, 12)


def draw_stash_queries(key, part):
    return query_draw(key, 21)


def draw_stash_kv(key, part):
    return pair_draw(key, 202, 22)


def set_ends(array, own_key, low, largest):
    longest = array.shape.index(max(array.shape))
    spots = []
    for shift in (0, 1):
        where = [jax.random.randint(jax.random.fold_in(own_key, axis), (), 0, length) for axis, length in enumerate(array.shape)]
        where[longest] = (where[longest] + shift) % array.shape[longest]
        spots.append(tuple(where))
    return array.at[spots[0]].set(low).at[spots[1]].set(largest)


def levels(key, extent, pieces, smallest, high):
    factor_of = 1.0
    for axis_at, shards_of in pieces:
        steps = jax.random.uniform(jax.random.fold_in(jax.random.fold_in(key, 6), axis_at), (shards_of,), jnp.float32, smallest / len(pieces), high / len(pieces))
        factor_of = factor_of * jnp.repeat(jnp.exp(steps), extent[axis_at] // shards_of).reshape((-1,) + (1,) * (len(extent) - 1 - axis_at))
    return factor_of


def normal_values(rng, dims, scale, most, cuts=(), held_as=jnp.bfloat16):
    factor_of = levels(rng, dims, cuts, -0.22, 0.18) if cuts else 1.0
    result = jax.random.normal(rng, dims, jnp.float32) * scale * factor_of
    return jnp.minimum(jnp.maximum(result, -most), most).astype(held_as)


def setup_inputs(seed: int = 0) -> dict:
    streams_of = jax.random.split(jax.random.key(seed), 10)
    return {
        "fwd_queries": draw_fwd_queries(jax.random.fold_in(streams_of[9], 71), 0),
        "fwd_kv": draw_fwd_kv(jax.random.fold_in(streams_of[9], 71), 0),
        "fwd_resid": normal_values(streams_of[2], (SECTIONS, TOK, D), 1.0, 6.0, ((0, 64), (2, 8))),
        "fwd_bounds": set_ends(jax.random.randint(streams_of[3], (SECTIONS,), 1, TOK), jax.random.fold_in(streams_of[3], 1), 1, TOK - 1).astype(jnp.int32),
        "gain": jnp.clip(1.0 + 0.18 * jax.random.normal(streams_of[4], (D,), jnp.float32), 0.099609375, 1.8984375).astype(jnp.bfloat16),
        "stash_queries": draw_stash_queries(jax.random.fold_in(streams_of[9], 71), 0),
        "stash_kv": draw_stash_kv(jax.random.fold_in(streams_of[9], 71), 0),
        "stash_bounds": set_ends(jax.random.randint(streams_of[7], (SECTIONS,), 1, TOK), jax.random.fold_in(streams_of[7], 1), 1, TOK - 1).astype(jnp.int32),
        "grad_out": normal_values(streams_of[8], (SECTIONS, TOK, D), 1.0, 6.0, ((0, 64), (2, 8))),
    }


def visible_mask(tok, bound):
    rows = jnp.arange(tok, dtype=jnp.int32)[:, None]
    cols = jnp.arange(tok, dtype=jnp.int32)[None, :]
    return (cols <= rows) & ((cols >= bound) | (rows < bound))

def split_heads(queries, pairs):
    tok = queries.shape[0]
    kv_heads = pairs.shape[2] // HD
    group = queries.shape[1] // HD // kv_heads
    q_heads = queries.reshape(tok, kv_heads, group, HD)
    k_heads = pairs[0].reshape(tok, kv_heads, HD)
    v_heads = pairs[1].reshape(tok, kv_heads, HD)
    return (q_heads, k_heads, v_heads)

def probs_of(q_heads, k_heads, bound):
    tok = q_heads.shape[0]
    scores = jnp.einsum('iagd,jad->agij', q_heads.astype(jnp.float32), k_heads.astype(jnp.float32))
    scores = scores * HD ** (-0.5)
    scores = jnp.where(visible_mask(tok, bound)[None, None], scores, -jnp.inf)
    top = lax.optimization_barrier(jnp.max(scores, axis=-1, keepdims=True))
    weights = jnp.exp(scores - top)
    return weights / lax.optimization_barrier(jnp.sum(weights, axis=-1, keepdims=True))

def forward_section(items):
    queries, pairs, resid, bound, gain = items
    q_heads, k_heads, v_heads = split_heads(queries, pairs)
    probs = probs_of(q_heads, k_heads, bound)
    rounded = probs.astype(jnp.bfloat16)
    mixed = jnp.einsum('agij,jad->iagd', rounded.astype(jnp.float32), v_heads.astype(jnp.float32))
    handoff = (resid.astype(jnp.float32) + mixed.reshape(resid.shape)).astype(jnp.bfloat16)
    handoff = lax.optimization_barrier(handoff).astype(jnp.float32)
    squares = lax.optimization_barrier(jnp.sum(handoff * handoff, axis=1))
    scale = lax.rsqrt(squares / D + 1e-05)
    return (handoff * scale[:, None] * gain.astype(jnp.float32)[None, :]).astype(jnp.bfloat16)

def backward_section(items):
    queries, pairs, bound, grads = items
    tok = queries.shape[0]
    q_heads, k_heads, v_heads = split_heads(queries, pairs)
    probs = probs_of(q_heads, k_heads, bound)
    rounded = probs.astype(jnp.bfloat16).astype(jnp.float32)
    g_heads = grads.reshape(q_heads.shape).astype(jnp.float32)
    grad_v = jnp.einsum('agij,iagd->jad', rounded, g_heads)
    grad_p = jnp.einsum('iagd,jad->agij', g_heads, v_heads.astype(jnp.float32))
    grad_s = probs * (grad_p - lax.optimization_barrier(jnp.sum(probs * grad_p, axis=-1, keepdims=True)))
    grad_s = (grad_s * HD ** (-0.5)).astype(jnp.bfloat16).astype(jnp.float32)
    grad_q = jnp.einsum('agij,jad->iagd', grad_s, k_heads.astype(jnp.float32))
    grad_k = jnp.einsum('agij,iagd->jad', grad_s, q_heads.astype(jnp.float32))
    grad_q = grad_q.reshape(tok, queries.shape[1]).astype(jnp.bfloat16)
    grad_pair = jnp.stack([grad_k.reshape(tok, -1), grad_v.reshape(tok, -1)]).astype(jnp.bfloat16)
    return (grad_q, grad_pair)

def reference(fwd_queries, fwd_kv, fwd_resid, fwd_bounds, gain, stash_queries, stash_kv, stash_bounds, grad_out):
    q_in = jnp.roll(fwd_queries, 1, axis=0)
    kv_in = jnp.roll(fwd_kv, 1, axis=0)
    r_in = jnp.roll(fwd_resid, 1, axis=0)
    b_in = jnp.roll(fwd_bounds, 1, axis=0)
    gains = jnp.broadcast_to(gain, (SECTIONS,) + gain.shape)
    normed = lax.map(forward_section, (q_in, kv_in, r_in, b_in, gains))
    half = SECTIONS // 2
    q_back = jnp.roll(stash_queries, half, axis=0)
    kv_back = jnp.roll(stash_kv, half, axis=0)
    b_back = jnp.roll(stash_bounds, half, axis=0)
    g_back = jnp.roll(grad_out, -1, axis=0)
    grad_queries, grad_kv = lax.map(backward_section, (q_back, kv_back, b_back, g_back))
    return (normed, grad_queries, grad_kv)
```

```python
import jax
import jax.numpy as jnp
from jax import lax
from jax.experimental import pallas as pl
from jax.experimental.pallas import tpu as pltpu
from jax.sharding import PartitionSpec as P

HD = 128
D = 8192
BLK = 128
LOG2E = 1.4426950408889634
NT = (((1,), (1,)), ((), ()))


def shifted(value, by):
    peers = lax.axis_size("pipe")
    return lax.ppermute(value, "pipe", [(i, (i + by) % peers) for i in range(peers)])


def partner(value):
    peers = lax.axis_size("pipe")
    return lax.ppermute(value, "pipe", [(i, i ^ (peers // 2)) for i in range(peers)])


def dot(a, b, dims=(((1,), (0,)), ((), ()))):
    return lax.dot_general(a, b, dims, preferred_element_type=jnp.float32)


def padded(block, rows):
    if block.shape[0] == rows:
        return block
    fill = jnp.zeros((rows - block.shape[0], block.shape[1]), block.dtype)
    return jnp.concatenate([block, fill], axis=0)


def bias_of(first, depth, bound):
    keys = lax.broadcasted_iota(jnp.int32, (depth, BLK), 0)
    rows = lax.broadcasted_iota(jnp.int32, (depth, BLK), 1) + first
    seen = (keys <= rows) & ((keys >= bound) | (rows < bound))
    return jnp.where(seen, 0.0, -jnp.inf).astype(jnp.float32)


def turned(block):
    return block.astype(jnp.float32).T.astype(jnp.bfloat16)


def probs_turned(keys, queries, bias):
    scores = dot(keys, queries, NT) + jnp.concatenate([bias, bias], axis=1)
    top = jnp.max(scores, axis=0, keepdims=True)
    weights = jnp.exp2((scores - top) * (LOG2E * HD**-0.5))
    return weights * (1.0 / jnp.sum(weights, axis=0, keepdims=True))


def stacked(ref, first, last):
    two = [padded(ref[first:last, h * HD : (h + 1) * HD], BLK) for h in range(2)]
    return jnp.concatenate(two, axis=0)


def spans(tok):
    return [(first, min(first + BLK, tok), first + BLK) for first in range(0, tok, BLK)]


def forward_kernel(b_ref, q_ref, kv_ref, r_ref, out_ref, sq_ref, k_pad, v_turned, bias_ref):
    tok = q_ref.shape[0]
    deep = k_pad.shape[0]

    @pl.when(pl.program_id(0) == 0)
    def _():
        k_pad[...] = padded(kv_ref[0], deep)
        v_turned[...] = turned(padded(kv_ref[1], deep))
        for n, (first, _, depth) in enumerate(spans(tok)):
            bias_ref[n, :depth] = bias_of(first, depth, b_ref[0])
        sq_ref[...] = jnp.zeros_like(sq_ref)

    for n, (first, last, depth) in enumerate(spans(tok)):
        probs = probs_turned(k_pad[:depth], stacked(q_ref, first, last), bias_ref[n, :depth])
        mixed = dot(v_turned[:, :depth], probs.astype(jnp.bfloat16))
        for h in range(2):
            cols = slice(h * HD, (h + 1) * HD)
            own = mixed[:, cols].T[: last - first]
            handoff = (r_ref[first:last, cols].astype(jnp.float32) + own).astype(jnp.bfloat16)
            out_ref[first:last, cols] = handoff
            wide = handoff.astype(jnp.float32)
            sq_ref[first:last] += wide * wide


def forward_local(queries, pairs, resid, bound):
    tok, width = queries.shape
    deep = -(-tok // BLK) * BLK
    two = pl.BlockSpec((tok, 2 * HD), lambda i: (0, i))
    return pl.pallas_call(
        forward_kernel,
        grid=(width // (2 * HD),),
        in_specs=[
            pl.BlockSpec(memory_space=pltpu.SMEM),
            two,
            pl.BlockSpec((2, tok, HD), lambda i: (0, 0, 0)),
            two,
        ],
        out_specs=[two, pl.BlockSpec((tok, HD), lambda i: (0, 0))],
        out_shape=[
            jax.ShapeDtypeStruct((tok, width), jnp.bfloat16),
            jax.ShapeDtypeStruct((tok, HD), jnp.float32),
        ],
        scratch_shapes=[
            pltpu.VMEM((deep, HD), jnp.bfloat16),
            pltpu.VMEM((HD, deep), jnp.bfloat16),
            pltpu.VMEM((deep // BLK, deep, BLK), jnp.float32),
        ],
        compiler_params=pltpu.CompilerParams(vmem_limit_bytes=32 * 2**20),
        cost_estimate=pl.CostEstimate(flops=6 * 10**8, bytes_accessed=3 * 10**6, transcendentals=10**6),
        name="forward",
    )(bound, queries, pairs, resid)


def backward_kernel(q_ref, kvb_ref, g_ref, dq_ref, dkv_ref, k_pad, v_pad, k_turned, bias_ref, dk_ref, dv_ref):
    tok = q_ref.shape[0]
    deep = k_pad.shape[0]

    @pl.when(pl.program_id(0) == 0)
    def _():
        k_pad[...] = padded(kvb_ref[:tok], deep)
        v_pad[...] = padded(kvb_ref[tok : 2 * tok], deep)
        k_turned[...] = turned(k_pad[...])
        digits = kvb_ref[2 * tok :].astype(jnp.float32)
        bound = (digits[0:1] * 16.0 + digits[8:9]).astype(jnp.int32)
        for n, (first, _, depth) in enumerate(spans(tok)):
            bias_ref[n, :depth] = bias_of(first, depth, bound)
        dk_ref[...] = jnp.zeros_like(dk_ref)
        dv_ref[...] = jnp.zeros_like(dv_ref)

    for n, (first, last, depth) in enumerate(spans(tok)):
        queries = stacked(q_ref, first, last)
        grads = stacked(g_ref, first, last)
        probs = probs_turned(k_pad[:depth], queries, bias_ref[n, :depth])
        dv_ref[:depth] += dot(probs.astype(jnp.bfloat16), grads)
        grad_p = dot(v_pad[:depth], grads, NT)
        total = jnp.sum(probs * grad_p, axis=0, keepdims=True)
        grad_s = (probs * (grad_p - total) * HD**-0.5).astype(jnp.bfloat16)
        dk_ref[:depth] += dot(grad_s, queries)
        grad_q = dot(k_turned[:, :depth], grad_s)
        for h in range(2):
            cols = slice(h * HD, (h + 1) * HD)
            dq_ref[first:last, cols] = grad_q[:, cols].T[: last - first].astype(jnp.bfloat16)

    @pl.when(pl.program_id(0) == pl.num_programs(0) - 1)
    def _():
        dkv_ref[0] = dk_ref[:tok].astype(jnp.bfloat16)
        dkv_ref[1] = dv_ref[:tok].astype(jnp.bfloat16)


def backward_local(queries, pairs_bound, grads):
    tok, width = queries.shape
    deep = -(-tok // BLK) * BLK
    two = pl.BlockSpec((tok, 2 * HD), lambda i: (0, i))
    return pl.pallas_call(
        backward_kernel,
        grid=(width // (2 * HD),),
        in_specs=[two, pl.BlockSpec(pairs_bound.shape, lambda i: (0, 0)), two],
        out_specs=[two, pl.BlockSpec((2, tok, HD), lambda i: (0, 0, 0))],
        out_shape=[
            jax.ShapeDtypeStruct((tok, width), jnp.bfloat16),
            jax.ShapeDtypeStruct((2, tok, HD), jnp.bfloat16),
        ],
        scratch_shapes=[
            pltpu.VMEM((deep, HD), jnp.bfloat16),
            pltpu.VMEM((deep, HD), jnp.bfloat16),
            pltpu.VMEM((HD, deep), jnp.bfloat16),
            pltpu.VMEM((deep // BLK, deep, BLK), jnp.float32),
            pltpu.VMEM((deep, HD), jnp.float32),
            pltpu.VMEM((deep, HD), jnp.float32),
        ],
        compiler_params=pltpu.CompilerParams(vmem_limit_bytes=32 * 2**20),
        cost_estimate=pl.CostEstimate(flops=15 * 10**8, bytes_accessed=3 * 10**6, transcendentals=10**6),
        name="backward",
    )(queries, pairs_bound, grads)


def with_bound(pairs, bound):
    high = lax.broadcasted_iota(jnp.int32, (16, HD), 0) < 8
    digits = jnp.where(high, bound[0] // 16, bound[0] % 16).astype(jnp.bfloat16)
    return jnp.concatenate([pairs.reshape(-1, HD), digits], axis=0)


def per_device(fwd_queries, fwd_kv, fwd_resid, fwd_bounds, gain, stash_queries, stash_kv, stash_bounds, grad_out):
    kept_q = partner(stash_queries[0])
    kept_kvb = partner(with_bound(stash_kv[0], stash_bounds))
    grads_in = shifted(grad_out[0], -1)
    handoff, squares = forward_local(fwd_queries[0], fwd_kv[0], fwd_resid[0], fwd_bounds)
    handed = shifted(handoff, 1)
    squares = lax.psum(jnp.sum(squares, axis=1), "tensor")
    scale = shifted(lax.rsqrt(squares / D + 1e-05), 1)
    normed = (handed.astype(jnp.float32) * scale[:, None] * gain.astype(jnp.float32)[None, :]).astype(jnp.bfloat16)
    grad_queries, grad_kv = backward_local(kept_q, kept_kvb, grads_in)
    return (normed[None], grad_queries[None], grad_kv[None])


def solution(mesh):
    placed = (
        P("pipe", None, "tensor"),
        P("pipe", None, None, "tensor"),
        P("pipe", None, "tensor"),
        P("pipe"),
        P("tensor"),
        P("pipe", None, "tensor"),
        P("pipe", None, None, "tensor"),
        P("pipe"),
        P("pipe", None, "tensor"),
    )
    return jax.shard_map(
        per_device,
        mesh=mesh,
        in_specs=placed,
        out_specs=(
            P("pipe", None, "tensor"),
            P("pipe", None, "tensor"),
            P("pipe", None, None, "tensor"),
        ),
        check_vma=False,
    )
```

```python
import jax
import jax.numpy as jnp
from jax import lax
from jax.experimental import pallas as pl
from jax.experimental.pallas import tpu as pltpu
from jax.sharding import PartitionSpec as P

HD = 128
D = 8192
BLK = 128
GROUP = 8
LOG2E = 1.4426950408889634
NT = (((1,), (1,)), ((), ()))


def shifted(value, by):
    peers = lax.axis_size("pipe")
    return lax.ppermute(value, "pipe", [(i, (i + by) % peers) for i in range(peers)])


def partner(value):
    peers = lax.axis_size("pipe")
    return lax.ppermute(value, "pipe", [(i, i ^ (peers // 2)) for i in range(peers)])


def dot(a, b, dims=(((1,), (0,)), ((), ()))):
    return lax.dot_general(a, b, dims, preferred_element_type=jnp.float32)


def padded(block, rows):
    if block.shape[0] == rows:
        return block
    fill = jnp.zeros((rows - block.shape[0], block.shape[1]), block.dtype)
    return jnp.concatenate([block, fill], axis=0)


def bias_of(first, depth, bound):
    keys = lax.broadcasted_iota(jnp.int32, (depth, BLK), 0)
    rows = lax.broadcasted_iota(jnp.int32, (depth, BLK), 1) + first
    seen = (keys <= rows) & ((keys >= bound) | (rows < bound))
    return jnp.where(seen, 0.0, -jnp.inf).astype(jnp.float32)


def turned(block):
    return block.astype(jnp.float32).T.astype(jnp.bfloat16)


def weights_turned(keys, queries, bias):
    scores = dot(keys, queries, NT) + jnp.concatenate([bias] * GROUP, axis=1)
    top = jnp.max(scores, axis=0, keepdims=True)
    weights = jnp.exp2((scores - top) * (LOG2E * HD**-0.5))
    return weights, 1.0 / jnp.sum(weights, axis=0, keepdims=True)


def stacked(ref, start, first, last):
    heads = [padded(ref[first:last, (start + h) * HD : (start + h + 1) * HD], BLK) for h in range(GROUP)]
    return jnp.concatenate(heads, axis=0)


def bodies(tok, width):
    spans = [(first, min(first + BLK, tok), first + BLK) for first in range(0, tok, BLK)]
    return [span + (start,) for span in reversed(spans) for start in range(0, width // HD, GROUP)]


def forward_kernel(b_ref, q_far, kv_far, r_far, out_ref, sq_ref, q_ref, kv_ref, r_ref, sems):
    tok, width = q_ref.shape
    deep = -(-tok // BLK) * BLK
    near = [(kv_far, kv_ref), (q_far, q_ref), (r_far, r_ref)]
    copies = [pltpu.make_async_copy(src, dst, sems.at[n]) for n, (src, dst) in enumerate(near)]
    for copy in copies:
        copy.start()
    for copy in copies:
        copy.wait()
    keys = padded(kv_ref[0], deep)
    values = turned(padded(kv_ref[1], deep))
    biases = {}
    squares = {}
    for first, last, depth, start in bodies(tok, width):
        if first not in biases:
            biases[first] = bias_of(first, depth, b_ref[0])
        weights, inverse = weights_turned(keys[:depth], stacked(q_ref, start, first, last), biases[first])
        mixed = dot(values[:, :depth], (weights * inverse).astype(jnp.bfloat16))
        for h in range(GROUP):
            cols = slice((start + h) * HD, (start + h + 1) * HD)
            own = mixed[:, h * BLK : (h + 1) * BLK].T[: last - first]
            handoff = (r_ref[first:last, cols].astype(jnp.float32) + own).astype(jnp.bfloat16)
            out_ref[first:last, cols] = handoff
            wide = handoff.astype(jnp.float32)
            squares[first] = squares.get(first, 0.0) + wide * wide
    for first, square in squares.items():
        sq_ref[first : first + square.shape[0]] = square


def forward_local(queries, pairs, resid, bound):
    tok, width = queries.shape
    whole = pl.BlockSpec(memory_space=pltpu.VMEM)
    far = pl.BlockSpec(memory_space=pltpu.HBM)
    return pl.pallas_call(
        forward_kernel,
        in_specs=[pl.BlockSpec(memory_space=pltpu.SMEM), far, far, far],
        out_specs=[whole, whole],
        out_shape=[
            jax.ShapeDtypeStruct((tok, width), jnp.bfloat16),
            jax.ShapeDtypeStruct((tok, HD), jnp.float32),
        ],
        scratch_shapes=[
            pltpu.VMEM(queries.shape, jnp.bfloat16),
            pltpu.VMEM(pairs.shape, jnp.bfloat16),
            pltpu.VMEM(resid.shape, jnp.bfloat16),
            pltpu.SemaphoreType.DMA((3,)),
        ],
        compiler_params=pltpu.CompilerParams(vmem_limit_bytes=32 * 2**20),
        cost_estimate=pl.CostEstimate(flops=10**6, bytes_accessed=10**5, transcendentals=0),
        name="forward",
    )(bound, queries, pairs, resid)


def backward_kernel(q_ref, kvb_ref, g_ref, dq_ref, dkv_ref, dk_ref, dv_ref):
    tok, width = q_ref.shape
    deep = -(-tok // BLK) * BLK
    keys = padded(kvb_ref[:tok], deep)
    values = padded(kvb_ref[tok : 2 * tok], deep)
    keys_turned = turned(keys)
    digits = kvb_ref[2 * tok :].astype(jnp.float32)
    bound = (digits[0:1] * 16.0 + digits[8:9]).astype(jnp.int32)
    biases = {}
    for n, (first, last, depth, start) in enumerate(bodies(tok, width)):
        if first not in biases:
            biases[first] = bias_of(first, depth, bound)
        queries = stacked(q_ref, start, first, last)
        grads = stacked(g_ref, start, first, last)
        weights, inverse = weights_turned(keys[:depth], queries, biases[first])
        probs = weights * inverse
        own_v = dot(probs.astype(jnp.bfloat16), grads)
        grad_p = dot(values[:depth], grads, NT)
        total = jnp.sum(probs * grad_p, axis=0, keepdims=True)
        grad_s = (probs * (grad_p - total) * HD**-0.5).astype(jnp.bfloat16)
        own_k = dot(grad_s, queries)
        if n == 0:
            dv_ref[:depth] = own_v
            dk_ref[:depth] = own_k
        else:
            dv_ref[:depth] += own_v
            dk_ref[:depth] += own_k
        grad_q = dot(keys_turned[:, :depth], grad_s)
        for h in range(GROUP):
            cols = slice((start + h) * HD, (start + h + 1) * HD)
            dq_ref[first:last, cols] = grad_q[:, h * BLK : (h + 1) * BLK].T[: last - first].astype(jnp.bfloat16)
    dkv_ref[0] = dk_ref[:tok].astype(jnp.bfloat16)
    dkv_ref[1] = dv_ref[:tok].astype(jnp.bfloat16)


def backward_local(queries, pairs_bound, grads):
    tok, width = queries.shape
    deep = -(-tok // BLK) * BLK
    whole = pl.BlockSpec(memory_space=pltpu.VMEM)
    return pl.pallas_call(
        backward_kernel,
        in_specs=[whole, whole, whole],
        out_specs=[whole, whole],
        out_shape=[
            jax.ShapeDtypeStruct((tok, width), jnp.bfloat16),
            jax.ShapeDtypeStruct((2, tok, HD), jnp.bfloat16),
        ],
        scratch_shapes=[
            pltpu.VMEM((deep, HD), jnp.float32),
            pltpu.VMEM((deep, HD), jnp.float32),
        ],
        compiler_params=pltpu.CompilerParams(vmem_limit_bytes=32 * 2**20),
        cost_estimate=pl.CostEstimate(flops=10**11, bytes_accessed=3 * 10**6, transcendentals=10**6),
        name="backward",
    )(queries, pairs_bound, grads)


def with_bound(pairs, bound):
    high = lax.broadcasted_iota(jnp.int32, (16, HD), 0) < 8
    digits = jnp.where(high, bound[0] >> 4, bound[0] & 15).astype(jnp.bfloat16)
    return jnp.concatenate([pairs.reshape(-1, HD), digits], axis=0)


def summed(squares):
    peers = lax.axis_size("tensor")
    parts = jnp.broadcast_to(squares[None], (peers,) + squares.shape)
    return jnp.sum(lax.all_to_all(parts, "tensor", 0, 0), axis=0)


def per_device(fwd_queries, fwd_kv, fwd_resid, fwd_bounds, gain, stash_queries, stash_kv, stash_bounds, grad_out):
    kept_q = partner(stash_queries[0])
    handoff, squares = forward_local(fwd_queries[0], fwd_kv[0], fwd_resid[0], fwd_bounds)
    squares, grad_out = lax.optimization_barrier((squares, grad_out))
    grads_in = shifted(grad_out[0], -1)
    handed = shifted(handoff, 1)
    kept_kvb = partner(with_bound(stash_kv[0], stash_bounds))
    scale = shifted(lax.rsqrt(summed(jnp.sum(squares, axis=1)) / D + 1e-05), 1)
    grad_queries, grad_kv = backward_local(kept_q, kept_kvb, grads_in)
    handed, scale, grad_kv = lax.optimization_barrier((handed, scale, grad_kv))
    normed = (handed.astype(jnp.float32) * scale[:, None] * gain.astype(jnp.float32)[None, :]).astype(jnp.bfloat16)
    return (normed[None], grad_queries[None], grad_kv[None])


def solution(mesh):
    placed = (
        P("pipe", None, "tensor"),
        P("pipe", None, None, "tensor"),
        P("pipe", None, "tensor"),
        P("pipe"),
        P("tensor"),
        P("pipe", None, "tensor"),
        P("pipe", None, None, "tensor"),
        P("pipe"),
        P("pipe", None, "tensor"),
    )
    return jax.shard_map(
        per_device,
        mesh=mesh,
        in_specs=placed,
        out_specs=(
            P("pipe", None, "tensor"),
            P("pipe", None, "tensor"),
            P("pipe", None, None, "tensor"),
        ),
        check_vma=False,
    )
```

```python
import jax
import jax.numpy as jnp
from jax import lax
from jax.experimental import pallas as pl
from jax.experimental.pallas import tpu as pltpu
from jax.sharding import PartitionSpec as P

HD = 128
D = 8192
BLK = 128
GROUP = 8
LOG2E = 1.4426950408889634
NT = (((1,), (1,)), ((), ()))


def shifted(value, by):
    peers = lax.axis_size("pipe")
    return lax.ppermute(value, "pipe", [(i, (i + by) % peers) for i in range(peers)])


def partner(value):
    peers = lax.axis_size("pipe")
    return lax.ppermute(value, "pipe", [(i, i ^ (peers // 2)) for i in range(peers)])


def dot(a, b, dims=(((1,), (0,)), ((), ()))):
    return lax.dot_general(a, b, dims, preferred_element_type=jnp.float32)


def padded(block, rows):
    if block.shape[0] == rows:
        return block
    fill = jnp.zeros((rows - block.shape[0], block.shape[1]), block.dtype)
    return jnp.concatenate([block, fill], axis=0)


def bias_of(first, depth, bound):
    keys = lax.broadcasted_iota(jnp.int32, (depth, BLK), 0)
    rows = lax.broadcasted_iota(jnp.int32, (depth, BLK), 1) + first
    seen = (keys <= rows) & ((keys >= bound) | (rows < bound))
    return jnp.where(seen, 0.0, -jnp.inf).astype(jnp.float32)


def turned(block):
    return block.astype(jnp.float32).T.astype(jnp.bfloat16)


def weights_turned(keys, queries, bias):
    scores = dot(keys, queries, NT) + jnp.concatenate([bias] * GROUP, axis=1)
    top = jnp.max(scores, axis=0, keepdims=True)
    weights = jnp.exp2((scores - top) * (LOG2E * HD**-0.5))
    return weights, 1.0 / jnp.sum(weights, axis=0, keepdims=True)


def stacked(ref, start, first, last):
    heads = [padded(ref[first:last, (start + h) * HD : (start + h + 1) * HD], BLK) for h in range(GROUP)]
    return jnp.concatenate(heads, axis=0)


def bodies(tok, width):
    spans = [(first, min(first + BLK, tok), first + BLK) for first in range(0, tok, BLK)]
    return [span + (start,) for span in reversed(spans) for start in range(0, width // HD, GROUP)]


def forward_kernel(b_ref, q_far, kv_far, r_far, out_ref, sq_ref, q_ref, kv_ref, r_ref, sems):
    tok, width = q_ref.shape
    deep = -(-tok // BLK) * BLK
    near = [(kv_far, kv_ref), (q_far, q_ref), (r_far, r_ref)]
    copies = [pltpu.make_async_copy(src, dst, sems.at[n]) for n, (src, dst) in enumerate(near)]
    for copy in copies:
        copy.start()
    for copy in copies:
        copy.wait()
    keys = padded(kv_ref[0], deep)
    values = turned(padded(kv_ref[1], deep))
    biases = {}
    squares = {}
    for first, last, depth, start in bodies(tok, width):
        if first not in biases:
            biases[first] = bias_of(first, depth, b_ref[0])
        weights, inverse = weights_turned(keys[:depth], stacked(q_ref, start, first, last), biases[first])
        mixed = dot(values[:, :depth], (weights * inverse).astype(jnp.bfloat16))
        for h in range(GROUP):
            cols = slice((start + h) * HD, (start + h + 1) * HD)
            own = mixed[:, h * BLK : (h + 1) * BLK].T[: last - first]
            handoff = (r_ref[first:last, cols].astype(jnp.float32) + own).astype(jnp.bfloat16)
            out_ref[first:last, cols] = handoff
            wide = handoff.astype(jnp.float32)
            squares[first] = squares.get(first, 0.0) + wide * wide
    for first, square in squares.items():
        sq_ref[first : first + square.shape[0]] = square


def forward_local(queries, pairs, resid, bound):
    tok, width = queries.shape
    whole = pl.BlockSpec(memory_space=pltpu.VMEM)
    far = pl.BlockSpec(memory_space=pltpu.HBM)
    return pl.pallas_call(
        forward_kernel,
        in_specs=[pl.BlockSpec(memory_space=pltpu.SMEM), far, far, far],
        out_specs=[whole, whole],
        out_shape=[
            jax.ShapeDtypeStruct((tok, width), jnp.bfloat16),
            jax.ShapeDtypeStruct((tok, HD), jnp.float32),
        ],
        scratch_shapes=[
            pltpu.VMEM(queries.shape, jnp.bfloat16),
            pltpu.VMEM(pairs.shape, jnp.bfloat16),
            pltpu.VMEM(resid.shape, jnp.bfloat16),
            pltpu.SemaphoreType.DMA((3,)),
        ],
        compiler_params=pltpu.CompilerParams(vmem_limit_bytes=32 * 2**20),
        cost_estimate=pl.CostEstimate(flops=10**6, bytes_accessed=10**5, transcendentals=0),
        name="forward",
    )(bound, queries, pairs, resid)


def backward_kernel(
    q_ref, kvb_ref, g_ref, dq_far, dkv_far, dq_ref, dkv_ref, dk_ref, dv_ref, sems
):
    tok, width = q_ref.shape
    deep = dk_ref.shape[0]
    blocks = [block[:3] for block in bodies(tok, width) if block[3] == 0]
    gone = []

    def leave(source, target):
        copy = pltpu.make_async_copy(source, target, sems.at[len(gone)])
        copy.start()
        gone.append(copy)

    keys = padded(kvb_ref[:tok], deep)
    values = padded(kvb_ref[tok : 2 * tok], deep)
    keys_turned = turned(keys)
    digits = kvb_ref[2 * tok :].astype(jnp.float32)
    bound = (digits[0:1] * 16.0 + digits[8:9]).astype(jnp.int32)
    for n, (first, last, depth) in enumerate(blocks):
        rows = pl.ds(first, last - first)
        bias = bias_of(first, depth, bound)
        for start in range(0, width // HD, GROUP):
            queries = stacked(q_ref, start, first, last)
            grads = stacked(g_ref, start, first, last)
            weights, inverse = weights_turned(keys[:depth], queries, bias)
            probs = weights * inverse
            own_v = dot(probs.astype(jnp.bfloat16), grads)
            grad_p = dot(values[:depth], grads, NT)
            total = jnp.sum(probs * grad_p, axis=0, keepdims=True)
            grad_s = (probs * (grad_p - total) * HD**-0.5).astype(jnp.bfloat16)
            own_k = dot(grad_s, queries)
            if n == 0 and start == 0:
                dv_ref[:depth] = own_v
                dk_ref[:depth] = own_k
            else:
                dv_ref[:depth] += own_v
                dk_ref[:depth] += own_k
            grad_q = dot(keys_turned[:, :depth], grad_s)
            for h in range(GROUP):
                cols = slice((start + h) * HD, (start + h + 1) * HD)
                dq_ref[first:last, cols] = grad_q[:, h * BLK : (h + 1) * BLK].T[: last - first].astype(jnp.bfloat16)
        dkv_ref[0, first:last] = dk_ref[first:last].astype(jnp.bfloat16)
        dkv_ref[1, first:last] = dv_ref[first:last].astype(jnp.bfloat16)
        leave(dq_ref.at[rows], dq_far.at[rows])
        leave(dkv_ref.at[:, rows], dkv_far.at[:, rows])
    for copy in gone:
        copy.wait()


def backward_local(queries, pairs_bound, grads):
    tok, width = queries.shape
    deep = -(-tok // BLK) * BLK
    whole = pl.BlockSpec(memory_space=pltpu.VMEM)
    far = pl.BlockSpec(memory_space=pl.ANY)
    return pl.pallas_call(
        backward_kernel,
        in_specs=[whole] * 3,
        out_specs=[far] * 2,
        out_shape=[
            jax.ShapeDtypeStruct((tok, width), jnp.bfloat16),
            jax.ShapeDtypeStruct((2, tok, HD), jnp.bfloat16),
        ],
        scratch_shapes=[
            pltpu.VMEM((tok, width), jnp.bfloat16),
            pltpu.VMEM((2, tok, HD), jnp.bfloat16),
            pltpu.VMEM((deep, HD), jnp.float32),
            pltpu.VMEM((deep, HD), jnp.float32),
            pltpu.SemaphoreType.DMA((2 * (deep // BLK),)),
        ],
        compiler_params=pltpu.CompilerParams(vmem_limit_bytes=32 * 2**20),
        cost_estimate=pl.CostEstimate(flops=10**11, bytes_accessed=3 * 10**6, transcendentals=10**6),
        name="backward",
    )(queries, pairs_bound, grads)


def with_bound(pairs, bound):
    high = lax.broadcasted_iota(jnp.int32, (16, HD), 0) < 8
    digits = jnp.where(high, bound[0] >> 4, bound[0] & 15).astype(jnp.bfloat16)
    return jnp.concatenate([pairs.reshape(-1, HD), digits], axis=0)


def finish_kernel(after_ref, handed_ref, scale_ref, gain_ref, far_ref, out_ref, sems):
    del after_ref
    tok = handed_ref.shape[0]
    factor = gain_ref[...].astype(jnp.float32)
    copies = []
    for n, first in enumerate(range(0, tok, BLK)):
        rows = slice(first, min(first + BLK, tok))
        wide = handed_ref[rows].astype(jnp.float32) * scale_ref[rows] * factor
        out_ref[rows] = wide.astype(jnp.bfloat16)
        there = pl.ds(first, rows.stop - first)
        copies.append(pltpu.make_async_copy(out_ref.at[there], far_ref.at[there], sems.at[n]))
        copies[-1].start()
    for copy in copies:
        copy.wait()


def finished(handed, scale, gain, after):
    whole = pl.BlockSpec(memory_space=pltpu.VMEM)
    return pl.pallas_call(
        finish_kernel,
        in_specs=[whole] * 4,
        out_specs=pl.BlockSpec(memory_space=pl.ANY),
        out_shape=jax.ShapeDtypeStruct(handed.shape, jnp.bfloat16),
        scratch_shapes=[
            pltpu.VMEM(handed.shape, jnp.bfloat16),
            pltpu.SemaphoreType.DMA((-(-handed.shape[0] // BLK),)),
        ],
        compiler_params=pltpu.CompilerParams(vmem_limit_bytes=16 * 2**20),
        cost_estimate=pl.CostEstimate(flops=10**9, bytes_accessed=0, transcendentals=0),
        name="finish",
    )(after, handed, scale, gain)


def summed(squares):
    peers = lax.axis_size("tensor")
    parts = jnp.broadcast_to(squares[None], (peers,) + squares.shape)
    return jnp.sum(lax.all_to_all(parts, "tensor", 0, 0), axis=0)


def per_device(fwd_queries, fwd_kv, fwd_resid, fwd_bounds, gain, stash_queries, stash_kv, stash_bounds, grad_out):
    kept_q = partner(stash_queries[0])
    handoff, squares = forward_local(fwd_queries[0], fwd_kv[0], fwd_resid[0], fwd_bounds)
    squares, grad_out = lax.optimization_barrier((squares, grad_out))
    grads_in = shifted(grad_out[0], -1)
    handed = shifted(handoff, 1)
    kept_kvb = partner(with_bound(stash_kv[0], stash_bounds))
    scale = shifted(lax.rsqrt(summed(jnp.sum(squares, axis=1)) / D + 1e-05), 1)
    normed = finished(handed, scale[:, None], gain[None], kept_q)
    normed, kept_kvb = lax.optimization_barrier((normed, kept_kvb))
    grad_queries, grad_kv = backward_local(kept_q, kept_kvb, grads_in)
    return (normed[None], grad_queries[None], grad_kv[None])


def solution(mesh):
    placed = (
        P("pipe", None, "tensor"),
        P("pipe", None, None, "tensor"),
        P("pipe", None, "tensor"),
        P("pipe"),
        P("tensor"),
        P("pipe", None, "tensor"),
        P("pipe", None, None, "tensor"),
        P("pipe"),
        P("pipe", None, "tensor"),
    )
    return jax.shard_map(
        per_device,
        mesh=mesh,
        in_specs=placed,
        out_specs=(
            P("pipe", None, "tensor"),
            P("pipe", None, "tensor"),
            P("pipe", None, None, "tensor"),
        ),
        check_vma=False,
    )
```

```python
import jax
import jax.numpy as jnp
from jax import lax
from jax.experimental import pallas as pl
from jax.experimental.pallas import tpu as pltpu
from jax.sharding import PartitionSpec as P

HD = 128
D = 8192
BLK = 128
GROUP = 8
LOG2E = 1.4426950408889634
NT = (((1,), (1,)), ((), ()))


def shifted(value, by):
    peers = lax.axis_size("pipe")
    return lax.ppermute(value, "pipe", [(i, (i + by) % peers) for i in range(peers)])


def partner(value):
    peers = lax.axis_size("pipe")
    return lax.ppermute(value, "pipe", [(i, i ^ (peers // 2)) for i in range(peers)])


def dot(a, b, dims=(((1,), (0,)), ((), ()))):
    return lax.dot_general(a, b, dims, preferred_element_type=jnp.float32)


def padded(block, rows):
    if block.shape[0] == rows:
        return block
    fill = jnp.zeros((rows - block.shape[0], block.shape[1]), block.dtype)
    return jnp.concatenate([block, fill], axis=0)


def bias_of(first, depth, bound):
    keys = lax.broadcasted_iota(jnp.int32, (depth, BLK), 0)
    rows = lax.broadcasted_iota(jnp.int32, (depth, BLK), 1) + first
    seen = (keys <= rows) & ((keys >= bound) | (rows < bound))
    return jnp.where(seen, 0.0, -jnp.inf).astype(jnp.float32)


def turned(block):
    return block.astype(jnp.float32).T.astype(jnp.bfloat16)


def weights_turned(keys, queries, bias):
    scores = dot(keys, queries, NT) + jnp.concatenate([bias] * GROUP, axis=1)
    top = jnp.max(scores, axis=0, keepdims=True)
    weights = jnp.exp2((scores - top) * (LOG2E * HD**-0.5))
    return weights, 1.0 / jnp.sum(weights, axis=0, keepdims=True)


def stacked(ref, start, first, last):
    heads = [padded(ref[first:last, (start + h) * HD : (start + h + 1) * HD], BLK) for h in range(GROUP)]
    return jnp.concatenate(heads, axis=0)


def bodies(tok, width):
    spans = [(first, min(first + BLK, tok), first + BLK) for first in range(0, tok, BLK)]
    return [span + (start,) for span in reversed(spans) for start in range(0, width // HD, GROUP)]


def forward_kernel(b_ref, q_far, kv_far, r_far, out_ref, sq_ref, q_ref, kv_ref, r_ref, sems):
    tok, width = q_ref.shape
    deep = -(-tok // BLK) * BLK
    near = [(kv_far, kv_ref), (q_far, q_ref), (r_far, r_ref)]
    copies = [pltpu.make_async_copy(src, dst, sems.at[n]) for n, (src, dst) in enumerate(near)]
    for copy in copies:
        copy.start()
    for copy in copies[:-1]:
        copy.wait()
    keys = padded(kv_ref[0], deep)
    values = turned(padded(kv_ref[1], deep))
    biases = {}
    squares = {}
    for first, last, depth, start in bodies(tok, width):
        if first not in biases:
            biases[first] = bias_of(first, depth, b_ref[0])
        weights, inverse = weights_turned(keys[:depth], stacked(q_ref, start, first, last), biases[first])
        mixed = dot(values[:, :depth], (weights * inverse).astype(jnp.bfloat16))
        if not squares:
            copies[-1].wait()
        for h in range(GROUP):
            cols = slice((start + h) * HD, (start + h + 1) * HD)
            own = mixed[:, h * BLK : (h + 1) * BLK].T[: last - first]
            handoff = (r_ref[first:last, cols].astype(jnp.float32) + own).astype(jnp.bfloat16)
            out_ref[first:last, cols] = handoff
            wide = handoff.astype(jnp.float32)
            squares[first] = squares.get(first, 0.0) + wide * wide
    for first, square in squares.items():
        sq_ref[first : first + square.shape[0]] = square


def forward_local(queries, pairs, resid, bound):
    tok, width = queries.shape
    whole = pl.BlockSpec(memory_space=pltpu.VMEM)
    far = pl.BlockSpec(memory_space=pltpu.HBM)
    return pl.pallas_call(
        forward_kernel,
        in_specs=[pl.BlockSpec(memory_space=pltpu.SMEM), far, far, far],
        out_specs=[whole, whole],
        out_shape=[
            jax.ShapeDtypeStruct((tok, width), jnp.bfloat16),
            jax.ShapeDtypeStruct((tok, HD), jnp.float32),
        ],
        scratch_shapes=[
            pltpu.VMEM(queries.shape, jnp.bfloat16),
            pltpu.VMEM(pairs.shape, jnp.bfloat16),
            pltpu.VMEM(resid.shape, jnp.bfloat16),
            pltpu.SemaphoreType.DMA((3,)),
        ],
        compiler_params=pltpu.CompilerParams(vmem_limit_bytes=56 * 2**20),
        cost_estimate=pl.CostEstimate(flops=10**6, bytes_accessed=10**5, transcendentals=0),
        name="forward",
    )(bound, queries, pairs, resid)


def backward_kernel(
    q_ref, kvb_ref, g_ref, dq_far, dkv_far, dq_ref, dkv_ref, dk_ref, dv_ref, sems
):
    tok, width = q_ref.shape
    deep = dk_ref.shape[0]
    blocks = [block[:3] for block in bodies(tok, width) if block[3] == 0]
    gone = []

    def leave(source, target):
        copy = pltpu.make_async_copy(source, target, sems.at[len(gone)])
        copy.start()
        gone.append(copy)

    keys = padded(kvb_ref[:tok], deep)
    values = padded(kvb_ref[tok : 2 * tok], deep)
    keys_turned = turned(keys)
    digits = kvb_ref[2 * tok :].astype(jnp.float32)
    bound = (digits[0:1] * 16.0 + digits[8:9]).astype(jnp.int32)
    for n, (first, last, depth) in enumerate(blocks):
        rows = pl.ds(first, last - first)
        bias = bias_of(first, depth, bound)
        for start in range(0, width // HD, GROUP):
            queries = stacked(q_ref, start, first, last)
            grads = stacked(g_ref, start, first, last)
            weights, inverse = weights_turned(keys[:depth], queries, bias)
            probs = weights * inverse
            own_v = dot(probs.astype(jnp.bfloat16), grads)
            grad_p = dot(values[:depth], grads, NT)
            total = jnp.sum(probs * grad_p, axis=0, keepdims=True)
            grad_s = (probs * (grad_p - total) * HD**-0.5).astype(jnp.bfloat16)
            own_k = dot(grad_s, queries)
            if n == 0 and start == 0:
                dv_ref[:depth] = own_v
                dk_ref[:depth] = own_k
            else:
                dv_ref[:depth] += own_v
                dk_ref[:depth] += own_k
            grad_q = dot(keys_turned[:, :depth], grad_s)
            for h in range(GROUP):
                cols = slice((start + h) * HD, (start + h + 1) * HD)
                dq_ref[first:last, cols] = grad_q[:, h * BLK : (h + 1) * BLK].T[: last - first].astype(jnp.bfloat16)
        dkv_ref[0, first:last] = dk_ref[first:last].astype(jnp.bfloat16)
        dkv_ref[1, first:last] = dv_ref[first:last].astype(jnp.bfloat16)
        leave(dq_ref.at[rows], dq_far.at[rows])
        leave(dkv_ref.at[:, rows], dkv_far.at[:, rows])
    for copy in gone:
        copy.wait()


def backward_local(queries, pairs_bound, grads):
    tok, width = queries.shape
    deep = -(-tok // BLK) * BLK
    whole = pl.BlockSpec(memory_space=pltpu.VMEM)
    far = pl.BlockSpec(memory_space=pl.ANY)
    return pl.pallas_call(
        backward_kernel,
        in_specs=[whole] * 3,
        out_specs=[far] * 2,
        out_shape=[
            jax.ShapeDtypeStruct((tok, width), jnp.bfloat16),
            jax.ShapeDtypeStruct((2, tok, HD), jnp.bfloat16),
        ],
        scratch_shapes=[
            pltpu.VMEM((tok, width), jnp.bfloat16),
            pltpu.VMEM((2, tok, HD), jnp.bfloat16),
            pltpu.VMEM((deep, HD), jnp.float32),
            pltpu.VMEM((deep, HD), jnp.float32),
            pltpu.SemaphoreType.DMA((2 * (deep // BLK),)),
        ],
        compiler_params=pltpu.CompilerParams(vmem_limit_bytes=32 * 2**20),
        cost_estimate=pl.CostEstimate(flops=10**11, bytes_accessed=3 * 10**6, transcendentals=10**6),
        name="backward",
    )(queries, pairs_bound, grads)


def with_bound(pairs, bound):
    high = lax.broadcasted_iota(jnp.int32, (16, HD), 0) < 8
    digits = jnp.where(high, bound[0] >> 4, bound[0] & 15).astype(jnp.bfloat16)
    return jnp.concatenate([pairs.reshape(-1, HD), digits], axis=0)


def finish_kernel(after_ref, handed_ref, scale_ref, gain_ref, far_ref, out_ref, sems):
    del after_ref
    tok = handed_ref.shape[0]
    factor = gain_ref[...].astype(jnp.float32)
    copies = []
    for n, first in enumerate(range(0, tok, BLK)):
        rows = slice(first, min(first + BLK, tok))
        wide = handed_ref[rows].astype(jnp.float32) * scale_ref[rows] * factor
        out_ref[rows] = wide.astype(jnp.bfloat16)
        there = pl.ds(first, rows.stop - first)
        copies.append(pltpu.make_async_copy(out_ref.at[there], far_ref.at[there], sems.at[n]))
        copies[-1].start()
    for copy in copies:
        copy.wait()


def finished(handed, scale, gain, after):
    whole = pl.BlockSpec(memory_space=pltpu.VMEM)
    return pl.pallas_call(
        finish_kernel,
        in_specs=[whole] * 4,
        out_specs=pl.BlockSpec(memory_space=pl.ANY),
        out_shape=jax.ShapeDtypeStruct(handed.shape, jnp.bfloat16),
        scratch_shapes=[
            pltpu.VMEM(handed.shape, jnp.bfloat16),
            pltpu.SemaphoreType.DMA((-(-handed.shape[0] // BLK),)),
        ],
        compiler_params=pltpu.CompilerParams(vmem_limit_bytes=16 * 2**20),
        cost_estimate=pl.CostEstimate(flops=10**9, bytes_accessed=0, transcendentals=0),
        name="finish",
    )(after, handed, scale, gain)


def summed(squares):
    peers = lax.axis_size("tensor")
    parts = jnp.broadcast_to(squares[None], (peers,) + squares.shape)
    return jnp.sum(lax.all_to_all(parts, "tensor", 0, 0), axis=0)


def per_device(fwd_queries, fwd_kv, fwd_resid, fwd_bounds, gain, stash_queries, stash_kv, stash_bounds, grad_out):
    kept_q = partner(stash_queries[0])
    handoff, squares = forward_local(fwd_queries[0], fwd_kv[0], fwd_resid[0], fwd_bounds)
    squares, grad_out = lax.optimization_barrier((squares, grad_out))
    grads_in = shifted(grad_out[0], -1)
    handed = shifted(handoff, 1)
    kept_kvb = partner(with_bound(stash_kv[0], stash_bounds))
    scale = shifted(lax.rsqrt(summed(jnp.sum(squares, axis=1)) / D + 1e-05), 1)
    normed = finished(handed, scale[:, None], gain[None], kept_q)
    normed, kept_kvb = lax.optimization_barrier((normed, kept_kvb))
    grad_queries, grad_kv = backward_local(kept_q, kept_kvb, grads_in)
    return (normed[None], grad_queries[None], grad_kv[None])


def solution(mesh):
    placed = (
        P("pipe", None, "tensor"),
        P("pipe", None, None, "tensor"),
        P("pipe", None, "tensor"),
        P("pipe"),
        P("tensor"),
        P("pipe", None, "tensor"),
        P("pipe", None, None, "tensor"),
        P("pipe"),
        P("pipe", None, "tensor"),
    )
    return jax.shard_map(
        per_device,
        mesh=mesh,
        in_specs=placed,
        out_specs=(
            P("pipe", None, "tensor"),
            P("pipe", None, "tensor"),
            P("pipe", None, None, "tensor"),
        ),
        check_vma=False,
    )
```

```python
import jax
import jax.numpy as jnp
from jax import lax
from jax.experimental import pallas as pl
from jax.experimental.pallas import tpu as pltpu
from jax.sharding import PartitionSpec as P

HD = 128
D = 8192
BLK = 128
GROUP = 8
STEP = 2
LOG2E = 1.4426950408889634
NT = (((1,), (1,)), ((), ()))


def shifted(value, by):
    peers = lax.axis_size("pipe")
    return lax.ppermute(value, "pipe", [(i, (i + by) % peers) for i in range(peers)])


def partner(value):
    peers = lax.axis_size("pipe")
    return lax.ppermute(value, "pipe", [(i, i ^ (peers // 2)) for i in range(peers)])


def dot(a, b, dims=(((1,), (0,)), ((), ()))):
    return lax.dot_general(a, b, dims, preferred_element_type=jnp.float32)


def padded(block, rows):
    if block.shape[0] == rows:
        return block
    fill = jnp.zeros((rows - block.shape[0], block.shape[1]), block.dtype)
    return jnp.concatenate([block, fill], axis=0)


def bias_of(first, depth, bound):
    keys = lax.broadcasted_iota(jnp.int32, (depth, BLK), 0)
    rows = lax.broadcasted_iota(jnp.int32, (depth, BLK), 1) + first
    seen = (keys <= rows) & ((keys >= bound) | (rows < bound))
    return jnp.where(seen, 0.0, -jnp.inf).astype(jnp.float32)


def turned(block):
    return block.astype(jnp.float32).T.astype(jnp.bfloat16)


def weights_of(scores):
    top = jnp.max(scores, axis=0, keepdims=True)
    weights = jnp.exp2((scores - top) * (LOG2E * HD**-0.5))
    return weights, 1.0 / jnp.sum(weights, axis=0, keepdims=True)


def weights_turned(keys, queries, bias):
    return weights_of(dot(keys, queries, NT) + jnp.concatenate([bias] * GROUP, axis=1))


def stacked(ref, start, first, last, group=GROUP):
    heads = [padded(ref[first:last, (start + h) * HD : (start + h + 1) * HD], BLK) for h in range(group)]
    return jnp.concatenate(heads, axis=0)


def bodies(tok, width):
    spans = [(first, min(first + BLK, tok), first + BLK) for first in range(0, tok, BLK)]
    return [span + (start,) for span in reversed(spans) for start in range(0, width // HD, GROUP)]


def forward_kernel(b_ref, q_far, kv_far, r_far, out_ref, sq_ref, q_ref, kv_ref, r_ref, sems):
    tok, width = q_ref.shape
    deep = -(-tok // BLK) * BLK
    near = [(kv_far, kv_ref), (q_far, q_ref), (r_far, r_ref)]
    copies = [pltpu.make_async_copy(src, dst, sems.at[n]) for n, (src, dst) in enumerate(near)]
    for copy in copies:
        copy.start()
    for copy in copies[:-1]:
        copy.wait()
    keys = padded(kv_ref[0], deep)
    values = turned(padded(kv_ref[1], deep))
    biases = {}
    squares = {}
    for first, last, depth, start in bodies(tok, width):
        if first not in biases:
            biases[first] = bias_of(first, depth, b_ref[0])
        weights, inverse = weights_turned(keys[:depth], stacked(q_ref, start, first, last), biases[first])
        mixed = dot(values[:, :depth], (weights * inverse).astype(jnp.bfloat16))
        if not squares:
            copies[-1].wait()
        for h in range(GROUP):
            cols = slice((start + h) * HD, (start + h + 1) * HD)
            own = mixed[:, h * BLK : (h + 1) * BLK].T[: last - first]
            handoff = (r_ref[first:last, cols].astype(jnp.float32) + own).astype(jnp.bfloat16)
            out_ref[first:last, cols] = handoff
            wide = handoff.astype(jnp.float32)
            squares[first] = squares.get(first, 0.0) + wide * wide
    for first, square in squares.items():
        sq_ref[first : first + square.shape[0]] = square


def forward_local(queries, pairs, resid, bound):
    tok, width = queries.shape
    whole = pl.BlockSpec(memory_space=pltpu.VMEM)
    far = pl.BlockSpec(memory_space=pltpu.HBM)
    return pl.pallas_call(
        forward_kernel,
        in_specs=[pl.BlockSpec(memory_space=pltpu.SMEM), far, far, far],
        out_specs=[whole, whole],
        out_shape=[
            jax.ShapeDtypeStruct((tok, width), jnp.bfloat16),
            jax.ShapeDtypeStruct((tok, HD), jnp.float32),
        ],
        scratch_shapes=[
            pltpu.VMEM(queries.shape, jnp.bfloat16),
            pltpu.VMEM(pairs.shape, jnp.bfloat16),
            pltpu.VMEM(resid.shape, jnp.bfloat16),
            pltpu.SemaphoreType.DMA((3,)),
        ],
        compiler_params=pltpu.CompilerParams(vmem_limit_bytes=56 * 2**20),
        cost_estimate=pl.CostEstimate(flops=10**6, bytes_accessed=10**5, transcendentals=0),
        name="forward",
    )(bound, queries, pairs, resid)


def backward_kernel(
    q_ref, kvb_ref, g_ref, dq_far, dkv_far, dq_ref, dkv_ref, dk_ref, dv_ref, sems
):
    tok, width = q_ref.shape
    deep = dk_ref.shape[0]
    blocks = [block[:3] for block in bodies(tok, width) if block[3] == 0]
    gone = []

    def leave(source, target):
        copy = pltpu.make_async_copy(source, target, sems.at[len(gone)])
        copy.start()
        gone.append(copy)

    keys = padded(kvb_ref[:tok], deep)
    values = padded(kvb_ref[tok : 2 * tok], deep)
    keys_turned = turned(keys)
    digits = kvb_ref[2 * tok :].astype(jnp.float32)
    bound = (digits[0:1] * 16.0 + digits[8:9]).astype(jnp.int32)
    steps = [block + (start,) for block in blocks for start in range(0, width // HD, STEP)]
    biases = {}

    def opened(step):
        first, last, depth, start = step
        if first not in biases:
            biases[first] = bias_of(first, depth, bound)
        queries = stacked(q_ref, start, first, last, STEP)
        grads = stacked(g_ref, start, first, last, STEP)
        scores = dot(keys[:depth], queries, NT) + jnp.concatenate([biases[first]] * STEP, axis=1)
        return queries, grads, scores, dot(values[:depth], grads, NT)

    ahead = opened(steps[0])
    for n, (first, last, depth, start) in enumerate(steps):
        queries, grads, scores, grad_p = ahead
        if n + 1 < len(steps):
            ahead = opened(steps[n + 1])
        weights, inverse = weights_of(scores)
        probs = weights * inverse
        own_v = dot(probs.astype(jnp.bfloat16), grads)
        total = jnp.sum(probs * grad_p, axis=0, keepdims=True)
        grad_s = (probs * (grad_p - total) * HD**-0.5).astype(jnp.bfloat16)
        own_k = dot(grad_s, queries)
        if n == 0:
            dv_ref[:depth] = own_v
            dk_ref[:depth] = own_k
        else:
            dv_ref[:depth] += own_v
            dk_ref[:depth] += own_k
        grad_q = dot(keys_turned[:, :depth], grad_s)
        for h in range(STEP):
            cols = slice((start + h) * HD, (start + h + 1) * HD)
            dq_ref[first:last, cols] = grad_q[:, h * BLK : (h + 1) * BLK].T[: last - first].astype(jnp.bfloat16)
        if start + STEP == width // HD:
            rows = pl.ds(first, last - first)
            dkv_ref[0, first:last] = dk_ref[first:last].astype(jnp.bfloat16)
            dkv_ref[1, first:last] = dv_ref[first:last].astype(jnp.bfloat16)
            leave(dq_ref.at[rows], dq_far.at[rows])
            leave(dkv_ref.at[:, rows], dkv_far.at[:, rows])
    for copy in gone:
        copy.wait()


def backward_local(queries, pairs_bound, grads):
    tok, width = queries.shape
    deep = -(-tok // BLK) * BLK
    whole = pl.BlockSpec(memory_space=pltpu.VMEM)
    far = pl.BlockSpec(memory_space=pl.ANY)
    return pl.pallas_call(
        backward_kernel,
        in_specs=[whole] * 3,
        out_specs=[far] * 2,
        out_shape=[
            jax.ShapeDtypeStruct((tok, width), jnp.bfloat16),
            jax.ShapeDtypeStruct((2, tok, HD), jnp.bfloat16),
        ],
        scratch_shapes=[
            pltpu.VMEM((tok, width), jnp.bfloat16),
            pltpu.VMEM((2, tok, HD), jnp.bfloat16),
            pltpu.VMEM((deep, HD), jnp.float32),
            pltpu.VMEM((deep, HD), jnp.float32),
            pltpu.SemaphoreType.DMA((2 * (deep // BLK),)),
        ],
        compiler_params=pltpu.CompilerParams(vmem_limit_bytes=32 * 2**20),
        cost_estimate=pl.CostEstimate(flops=10**11, bytes_accessed=3 * 10**6, transcendentals=10**6),
        name="backward",
    )(queries, pairs_bound, grads)


def with_bound(pairs, bound):
    high = lax.broadcasted_iota(jnp.int32, (16, HD), 0) < 8
    digits = jnp.where(high, bound[0] >> 4, bound[0] & 15).astype(jnp.bfloat16)
    return jnp.concatenate([pairs.reshape(-1, HD), digits], axis=0)


def finish_kernel(after_ref, handed_ref, scale_ref, gain_ref, far_ref, out_ref, sems):
    del after_ref
    tok = handed_ref.shape[0]
    factor = gain_ref[...].astype(jnp.float32)
    copies = []
    for n, first in enumerate(range(0, tok, BLK)):
        rows = slice(first, min(first + BLK, tok))
        wide = handed_ref[rows].astype(jnp.float32) * scale_ref[rows] * factor
        out_ref[rows] = wide.astype(jnp.bfloat16)
        there = pl.ds(first, rows.stop - first)
        copies.append(pltpu.make_async_copy(out_ref.at[there], far_ref.at[there], sems.at[n]))
        copies[-1].start()
    for copy in copies:
        copy.wait()


def finished(handed, scale, gain, after):
    whole = pl.BlockSpec(memory_space=pltpu.VMEM)
    return pl.pallas_call(
        finish_kernel,
        in_specs=[whole] * 4,
        out_specs=pl.BlockSpec(memory_space=pl.ANY),
        out_shape=jax.ShapeDtypeStruct(handed.shape, jnp.bfloat16),
        scratch_shapes=[
            pltpu.VMEM(handed.shape, jnp.bfloat16),
            pltpu.SemaphoreType.DMA((-(-handed.shape[0] // BLK),)),
        ],
        compiler_params=pltpu.CompilerParams(vmem_limit_bytes=16 * 2**20),
        cost_estimate=pl.CostEstimate(flops=10**9, bytes_accessed=0, transcendentals=0),
        name="finish",
    )(after, handed, scale, gain)


def summed(squares):
    peers = lax.axis_size("tensor")
    parts = jnp.broadcast_to(squares[None], (peers,) + squares.shape)
    return jnp.sum(lax.all_to_all(parts, "tensor", 0, 0), axis=0)


def per_device(fwd_queries, fwd_kv, fwd_resid, fwd_bounds, gain, stash_queries, stash_kv, stash_bounds, grad_out):
    kept_q = partner(stash_queries[0])
    handoff, squares = forward_local(fwd_queries[0], fwd_kv[0], fwd_resid[0], fwd_bounds)
    squares, grad_out = lax.optimization_barrier((squares, grad_out))
    grads_in = shifted(grad_out[0], -1)
    handed = shifted(handoff, 1)
    kept_kvb = partner(with_bound(stash_kv[0], stash_bounds))
    scale = shifted(lax.rsqrt(summed(jnp.sum(squares, axis=1)) / D + 1e-05), 1)
    normed = finished(handed, scale[:, None], gain[None], kept_q)
    normed, kept_kvb = lax.optimization_barrier((normed, kept_kvb))
    grad_queries, grad_kv = backward_local(kept_q, kept_kvb, grads_in)
    return (normed[None], grad_queries[None], grad_kv[None])


def solution(mesh):
    placed = (
        P("pipe", None, "tensor"),
        P("pipe", None, None, "tensor"),
        P("pipe", None, "tensor"),
        P("pipe"),
        P("tensor"),
        P("pipe", None, "tensor"),
        P("pipe", None, None, "tensor"),
        P("pipe"),
        P("pipe", None, "tensor"),
    )
    return jax.shard_map(
        per_device,
        mesh=mesh,
        in_specs=placed,
        out_specs=(
            P("pipe", None, "tensor"),
            P("pipe", None, "tensor"),
            P("pipe", None, None, "tensor"),
        ),
        check_vma=False,
    )
```
